512 devices in a mesh: inst: 8 (over x_hi, y), space: 64 (over z, x_lo, core).
Axes of the slice: x: 4 (x_hi: 2, x_lo: 2; x = x_hi * 2 + x_lo), y: 4, z: 16, core: 2. Of those that a mesh axis runs over, the one named last changes fastest.
Arguments:
- adjoint_start: float32 [32, 5, 64, 8, 128], P('inst', None, 'space'), may hold values from -4 to 4
- objective_gradient: float32 [32, 5, 64, 8, 128], P('inst', None, 'space'), may hold values from -24 to 24
- diag_block: bfloat16 [32, 5, 5, 64, 8, 128], P('inst', None, None, 'space'), may hold values from -1.25 to 8
- precond_inverse: bfloat16 [32, 5, 5, 64, 8, 128], P('inst', None, None, 'space'), may hold values from -0.0625 to 0.165
- jac_span: bfloat16 [32, 5, 5, 64, 8, 128], P('inst', None, None, 'space'), may hold values from -3 to 3
- jac_normal: bfloat16 [32, 5, 5, 64, 8, 128], P('inst', None, None, 'space'), may hold values from -3 to 3
- jac_chord: bfloat16 [32, 5, 5, 64, 8, 128], P('inst', None, None, 'space'), may hold values from -3 to 3
- colour: int32 [64, 8, 128], P('space'), may hold values from 0 to 3
- wall_vector: float32 [32, 5, 64, 128], P('inst', None, 'space'), may hold values from -0.9 to 0.9
- section_owner: int32 [64, 128], P('space'), may hold values from 0 to 511
Outputs:
- adjoint_out: float32 [32, 5, 64, 8, 128], P('inst', None, 'space')
- section_sens: float32 [32, 512], P('inst', 'space')
The draws below stay inside these ranges and needn't reach their ends.
All inputs are finite; a program needn't handle non-finite values.
Results may differ from the reference program's by a relative error of at most 0.0003.
Values sent between devices are 32-bit elements; how exact they have to be, the bound alone decides.
A program may use at most 64 MiB of HBM per device.

```python
import math
import jax
import jax.numpy as jnp
from jax import lax

SX = 1
SN = 8
SC = 128
NCOL = 4
SWEEPS = 2
PSTEPS = 2
NINST = 32
NX = 64
NSEC = 512


def block_draw(key, centre_low, centre_high, spread):
    shape = (NINST, 5, 5, NX, SN, SC)
    centre_key, side_key = jax.random.split(key)
    centre = jax.random.uniform(centre_key, shape, jnp.float32, centre_low, centre_high)
    side = spread * jax.random.uniform(side_key, shape, jnp.float32, -1.0, 1.0)
    row_index = lax.broadcasted_iota(jnp.int32, shape, 1)
    column_index = lax.broadcasted_iota(jnp.int32, shape, 2)
    return jnp.where(row_index == column_index, centre, side)


def draw_diag_block(key, part):
    key = jax.random.fold_in(key, 11)
    return block_draw(key, 5.0, 8.0, 1.2).astype(jnp.bfloat16)


def draw_precond_inverse(key, part):
    key = jax.random.fold_in(key, 23)
    return block_draw(key, 0.1, 0.16, 0.06).astype(jnp.bfloat16)


def with_ends(values, stream_key, low, high):
    longest = values.shape.index(max(values.shape))
    spots = []
    for shift in (0, 1):
        where = [jax.random.randint(jax.random.fold_in(stream_key, axis), (), 0, length) for axis, length in enumerate(values.shape)]
        where[longest] = (where[longest] + shift) % values.shape[longest]
        spots.append(tuple(where))
    return values.at[spots[0]].set(low).at[spots[1]].set(high)


def block_levels(own_key, dims, pieces, low, high):
    loudness, own = 1.0, jax.random.fold_in(own_key, 6)
    for axis_at, parts in pieces:
        draws = jnp.exp(jax.random.uniform(jax.random.fold_in(own, axis_at), (parts,), jnp.float32, low / len(pieces), high / len(pieces)))
        loudness = loudness * jnp.repeat(draws, dims[axis_at] // parts).reshape([-1 if axis == axis_at else 1 for axis in range(len(dims))])
    return loudness


def bell_draw(key, shape, scale, most, cuts=(), kind=jnp.bfloat16):
    result = jax.random.normal(key, shape, jnp.float32) * scale
    if len(cuts) > 0:
        result = block_levels(key, shape, cuts, -0.22, 0.18) * result
    return jnp.clip(result, min=-most, max=most).astype(kind)


def setup_inputs(seed: int = 0) -> dict:
    key_list = jax.random.split(jax.random.key(seed), 11)
    return {
        "adjoint_start": bell_draw(key_list[0], (NINST, 5, NX, SN, SC), 0.5, 4.0, ((0, 8), (2, 64)), jnp.float32),
        "objective_gradient": bell_draw(key_list[1], (NINST, 5, NX, SN, SC), 4.0, 24.0, ((0, 8), (2, 64)), jnp.float32),
        "diag_block": draw_diag_block(jax.random.fold_in(key_list[10], 71), 0),
        "precond_inverse": draw_precond_inverse(jax.random.fold_in(key_list[10], 71), 0),
        "jac_span": bell_draw(key_list[4], (NINST, 5, 5, NX, SN, SC), 0.5, 3.0, ((0, 8), (3, 64))),
        "jac_normal": bell_draw(key_list[5], (NINST, 5, 5, NX, SN, SC), 0.5, 3.0, ((0, 8), (3, 64))),
        "jac_chord": bell_draw(key_list[6], (NINST, 5, 5, NX, SN, SC), 0.5, 3.0, ((0, 8), (3, 64))),
        "colour": with_ends(jax.random.randint(key_list[7], (NX, SN, SC), 0, NCOL), jax.random.fold_in(key_list[7], 1), 0, NCOL - 1).astype(jnp.int32),
        "wall_vector": bell_draw(key_list[8], (NINST, 5, NX, SC), 0.15, 0.9, ((0, 8), (2, 64)), jnp.float32),
        "section_owner": with_ends(jax.random.randint(key_list[9], (NX, SC), 0, NSEC), jax.random.fold_in(key_list[9], 1), 0, NSEC - 1).astype(jnp.int32),
    }


spectral_gain = 0.25


def spectral_table(instances_all):
    table_rows = []
    for row_index in range(instances_all):
        row_values = []
        for col_index in range(instances_all):
            offset_gap = col_index - row_index
            if offset_gap == 0:
                row_values.append(0.0)
            else:
                parity_sign = 1.0 if offset_gap % 2 == 0 else -1.0
                row_values.append(spectral_gain * 0.5 * parity_sign / math.tan(math.pi * offset_gap / instances_all))
        table_rows.append(row_values)
    return table_rows


def apply_block(blocks, values_in):
    return jnp.sum(blocks.astype(jnp.float32) * values_in[:, None], axis=2)


def coupling(jac_span, jac_normal, jac_chord, values_in, minus_span, plus_span):
    zeros_rim = jnp.zeros_like(values_in[:, :, :, :1])
    minus_normal = jnp.concatenate([zeros_rim, values_in[:, :, :, :-1]], axis=3)
    plus_normal = jnp.concatenate([values_in[:, :, :, 1:], zeros_rim], axis=3)
    minus_chord = jnp.roll(values_in, 1, axis=4)
    plus_chord = jnp.roll(values_in, -1, axis=4)
    running = apply_block(jac_span, minus_span - plus_span)
    running = running + apply_block(jac_normal, minus_normal - plus_normal)
    running = running + apply_block(jac_chord, minus_chord - plus_chord)
    return 0.5 * running


def span_neighbours(current, frozen, slab_width):
    zeros_rim = jnp.zeros_like(current[:, :, :1])
    minus_now = jnp.concatenate([zeros_rim, current[:, :, :-1]], axis=2)
    plus_now = jnp.concatenate([current[:, :, 1:], zeros_rim], axis=2)
    minus_old = jnp.concatenate([zeros_rim, frozen[:, :, :-1]], axis=2)
    plus_old = jnp.concatenate([frozen[:, :, 1:], zeros_rim], axis=2)
    positions = jnp.arange(current.shape[2], dtype=jnp.int32) % slab_width
    lower_rim = (positions == 0)[:, None, None]
    upper_rim = (positions == slab_width - 1)[:, None, None]
    return jnp.where(lower_rim, minus_old, minus_now), jnp.where(upper_rim, plus_old, plus_now)


def local_residual(operands):
    adjoint, diagonal, jac_span, jac_normal, jac_chord = [item[None] for item in operands]
    minus_span, plus_span = span_neighbours(adjoint, adjoint, SX)
    return (apply_block(diagonal, adjoint) + coupling(jac_span, jac_normal, jac_chord, adjoint, minus_span, plus_span))[0]


def make_sweeps(colour):
    def instance_sweeps(operands):
        right_side, inverse, jac_span, jac_normal, jac_chord = [item[None] for item in operands]
        update = jnp.zeros_like(right_side)
        for sweep_index in range(SWEEPS):
            frozen = update
            if sweep_index % 2 == 0:
                colour_order = list(range(NCOL))
            else:
                colour_order = list(range(NCOL - 1, -1, -1))
            for colour_value in colour_order:
                minus_span, plus_span = span_neighbours(update, frozen, SX)
                updated = apply_block(inverse, right_side - coupling(jac_span, jac_normal, jac_chord, update, minus_span, plus_span))
                update = jnp.where(colour == colour_value, updated, update)
        return update[0]
    return instance_sweeps


def reference(adjoint_start, objective_gradient, diag_block, precond_inverse, jac_span, jac_normal, jac_chord, colour, wall_vector, section_owner):
    coefficients = jnp.asarray(spectral_table(NINST), jnp.float32)
    adjoint = adjoint_start
    sweeper = make_sweeps(colour)
    for pseudo_step in range(PSTEPS):
        spectral = jnp.einsum('mn,nkxyz->mkxyz', coefficients, adjoint, precision=lax.Precision.HIGHEST)
        local_part = lax.map(local_residual, (adjoint, diag_block, jac_span, jac_normal, jac_chord))
        right_side = objective_gradient - (local_part + spectral)
        update = lax.map(sweeper, (right_side, precond_inverse, jac_span, jac_normal, jac_chord))
        adjoint = adjoint + update
    wall_term = jnp.sum(wall_vector * adjoint[:, :, :, 0, :], axis=1)
    owners = section_owner.reshape(-1)
    one_hot = (owners[:, None] == jnp.arange(NSEC, dtype=jnp.int32)[None, :]).astype(jnp.float32)
    section_sens = jnp.dot(wall_term.reshape(NINST, -1), one_hot, precision=lax.Precision.HIGHEST, preferred_element_type=jnp.float32)
    return adjoint, section_sens
```

```python
import functools
import math

import jax
import jax.numpy as jnp
from jax import lax
from jax.experimental import pallas as pl
from jax.experimental.pallas import tpu as pltpu
from jax.sharding import PartitionSpec as P

NCOL = 4
PSTEPS = 2
SEC_DEV = 8
GAIN = 0.25
K = 5
MESH = pl.DeviceIdType.MESH


def spectral_row(count):
    row = [0.0]
    for gap in range(1, count):
        sign = 1.0 if gap % 2 == 0 else -1.0
        row.append(GAIN * 0.5 * sign / math.tan(math.pi * gap / count))
    return row


def ring_order(count):
    half = count // 2
    order = [half]
    for step in range(1, half + 1):
        for offset in (half - step, half + step):
            if 0 <= offset < count:
                order.append(offset)
    return order


def kernel(
    sizes,
    a_hbm, g_hbm, d_hbm, p_hbm, js_hbm, jn_hbm, jc_hbm, col_hbm, wall_hbm, own_hbm,
    adj_hbm, sens_ref,
    a_ref, a1_ref, g_ref, col_ref, wall_ref, own_ref, raw,
    dm, pm, jsm, jnm, jcm, ps, pn, pc,
    rs, b_ref, u_ref, h_ref, spec_rx, halo_rx, dest_hot, sec_tx, sec_rx,
    in_sem, spec_tx_sem, spec_rx_sem, halo_tx_sem, halo_rx_sem, sec_sem, out_sem,
):
    members, n_inst, n_space, quads = sizes
    row = spectral_row(members * n_inst)
    inst = lax.axis_index("inst")
    space = lax.axis_index("space")

    spec_peers = [(lax.rem(inst + d, n_inst), space) for d in range(1, n_inst)]
    halo_peers = [(inst, lax.rem(space + 1, n_space)), (inst, lax.rem(space + n_space - 1, n_space))]
    rings = n_space // quads
    zed, quad = space // quads, lax.rem(space, quads)
    sec_peers = []
    for dz in ring_order(rings):
        for dq in range(quads):
            if dz or dq:
                sec_peers.append((inst, lax.rem(zed + dz, rings) * quads + lax.rem(quad + dq, quads)))

    barrier = pltpu.get_barrier_semaphore()
    for peer in spec_peers + sec_peers:
        pl.semaphore_signal(barrier, inc=1, device_id=peer, device_id_type=MESH)
    loads = [
        pltpu.make_async_copy(src, dst, in_sem.at[n])
        for n, (src, dst) in enumerate(
            [
                (a_hbm, a_ref), (g_hbm, g_ref), (col_hbm, col_ref), (wall_hbm, wall_ref), (own_hbm, own_ref),
                (p_hbm, raw.at[0]), (jn_hbm, raw.at[1]), (jc_hbm, raw.at[2]), (js_hbm, raw.at[3]), (d_hbm, raw.at[4]),
            ]
        )
    ]
    for load in loads:
        load.start()
    loads[0].wait()
    pl.semaphore_wait(barrier, len(spec_peers) + len(sec_peers))

    def send_state(step, source):
        spec = []
        for e, peer in enumerate(spec_peers):
            copy = pltpu.make_async_remote_copy(
                src_ref=source, dst_ref=spec_rx.at[step, e], send_sem=spec_tx_sem.at[step, e],
                recv_sem=spec_rx_sem.at[step, e], device_id=peer, device_id_type=MESH,
            )
            copy.start()
            spec.append(copy)
        return spec

    def send_halo(slot, source):
        halo = []
        for side, peer in enumerate(halo_peers):
            copy = pltpu.make_async_remote_copy(
                src_ref=source, dst_ref=halo_rx.at[slot, side], send_sem=halo_tx_sem.at[slot, side],
                recv_sem=halo_rx_sem.at[slot, side], device_id=peer, device_id_type=MESH,
            )
            copy.start()
            halo.append(copy)
        return halo

    def block(ref, m, k, l):
        at = (m * K * K + k * K + l) * 8
        if not isinstance(at, int):
            at = pl.multiple_of(at, 8)
        return ref[pl.ds(at, 8), :]

    lane_row = lax.broadcasted_iota(jnp.int32, (8, 128), 0)

    def normal_diff(v):
        minus = jnp.where(lane_row > 0, pltpu.roll(v, 1, 0), 0.0)
        plus = jnp.where(lane_row < 7, pltpu.roll(v, 7, 0), 0.0)
        return minus - plus

    def chord_diff(v):
        return pltpu.roll(v, 1, 1) - pltpu.roll(v, 127, 1)

    def span_diff(slot, m, l):
        minus = jnp.where(space > 0, halo_rx[slot, 0, m, l], 0.0)
        plus = jnp.where(space < n_space - 1, halo_rx[slot, 1, m, l], 0.0)
        return minus - plus

    state = a_ref
    halo_a = send_halo(0, state)
    spec = send_state(0, state)

    for load in loads[1:]:
        load.wait()
    rows = members * K * K * 8
    part = 160
    for n, wide in enumerate((pm, jnm, jcm, jsm, dm)):
        @pl.loop(0, rows // part)
        def _(i, n=n, wide=wide):
            at = pl.multiple_of(i * part, part)
            wide[pl.ds(at, part), :] = raw[n, pl.ds(at, part), :].astype(jnp.float32)

    @pl.loop(0, members)
    def _(m):
        for jac, product in ((jnm, pn), (jcm, pc), (jsm, ps)):
            right = [[0.5 * block(jac, m, j, l) for l in range(K)] for j in range(K)]
            for k in range(K):
                left = [block(pm, m, k, j) for j in range(K)]
                for l in range(K):
                    total = left[0] * right[0][l]
                    for j in range(1, K):
                        total = total + left[j] * right[j][l]
                    at = pl.multiple_of((m * K * K + k * K + l) * 8, 8)
                    product[pl.ds(at, 8), :] = total

    owner = own_ref[...]
    dest_hot[...] = jnp.where(
        lax.broadcasted_iota(jnp.int32, (n_space, 128), 0) == jnp.broadcast_to(owner // SEC_DEV, (n_space, 128)), 1.0, 0.0
    ).astype(jnp.bfloat16)
    sec_tx[...] = jnp.zeros_like(sec_tx)
    colour = col_ref[...]

    for step in range(PSTEPS):
        @pl.loop(0, members)
        def _(m, state=state):
            v = [state[m, l] for l in range(K)]
            dn = [normal_diff(v[l]) for l in range(K)]
            dc = [chord_diff(v[l]) for l in range(K)]
            for k in range(K):
                local = block(dm, m, k, 0) * v[0]
                cross = block(jnm, m, k, 0) * dn[0] + block(jcm, m, k, 0) * dc[0]
                for l in range(1, K):
                    local = local + block(dm, m, k, l) * v[l]
                    cross = cross + (block(jnm, m, k, l) * dn[l] + block(jcm, m, k, l) * dc[l])
                rs[m, k] = g_ref[m, k] - (local + 0.5 * cross)

        def add_block(d, source):
            for k in range(K):
                v = [source[j, k] for j in range(members)]
                for m in range(members):
                    total = rs[m, k]
                    for j in range(members):
                        weight = row[(members * d + j - m) % len(row)]
                        if weight:
                            total = total - weight * v[j]
                    rs[m, k] = total

        add_block(0, state)
        for copy in halo_a:
            copy.wait_recv()

        @pl.loop(0, members)
        def _(m, step=step):
            ds = [span_diff(2 * step, m, l) for l in range(K)]
            for k in range(K):
                cross = block(jsm, m, k, 0) * ds[0]
                for l in range(1, K):
                    cross = cross + block(jsm, m, k, l) * ds[l]
                rs[m, k] = rs[m, k] - 0.5 * cross

        for e, copy in enumerate(spec):
            copy.wait_recv()
            add_block(n_inst - 1 - e, spec_rx.at[step, e])

        for m in range(members):
            r = [rs[m, l] for l in range(K)]
            for k in range(K):
                total = block(pm, m, k, 0) * r[0]
                for l in range(1, K):
                    total = total + block(pm, m, k, l) * r[l]
                b_ref[m, k] = total
                u_ref[m, k] = jnp.where(colour == 0, total, 0.0)

        def cross_terms(m, source):
            v = [source[m, l] for l in range(K)]
            dn = [normal_diff(v[l]) for l in range(K)]
            dc = [chord_diff(v[l]) for l in range(K)]
            out = []
            for k in range(K):
                total = block(pn, m, k, 0) * dn[0] + block(pc, m, k, 0) * dc[0]
                for l in range(1, K):
                    total = total + (block(pn, m, k, l) * dn[l] + block(pc, m, k, l) * dc[l])
                out.append(total)
            return v, out

        @pl.loop(1, NCOL)
        def _(value):
            mine = colour == value
            for m in range(members):
                v, cross = cross_terms(m, u_ref)
                for k in range(K):
                    u_ref[m, k] = jnp.where(mine, b_ref[m, k] - cross[k], v[k])

        halo_u = send_halo(2 * step + 1, u_ref)
        for m in range(members):
            _, cross = cross_terms(m, u_ref)
            for k in range(K):
                rs[m, k] = cross[k]
        for copy in halo_u:
            copy.wait_recv()
        for m in range(members):
            ds = [span_diff(2 * step + 1, m, l) for l in range(K)]
            for k in range(K):
                total = b_ref[m, k]
                for l in range(K):
                    total = total - block(ps, m, k, l) * ds[l]
                b_ref[m, k] = total
                h_ref[m, k] = jnp.where(colour == NCOL - 1, total - rs[m, k], u_ref[m, k])

        @pl.loop(1, NCOL)
        def _(back):
            mine = colour == NCOL - 1 - back
            for m in range(members):
                v, cross = cross_terms(m, h_ref)
                for k in range(K):
                    h_ref[m, k] = jnp.where(mine, b_ref[m, k] - cross[k], v[k])

        sent = spec + halo_a + halo_u
        if step < PSTEPS - 1:
            for m in range(members):
                for k in range(K):
                    a1_ref[m, k] = state[m, k] + h_ref[m, k]
            halo_a = send_halo(2 * step + 2, a1_ref)
            spec = send_state(step + 1, a1_ref)
            state = a1_ref
        else:
            for m in range(members):
                for k in range(K):
                    h_ref[m, k] = state[m, k] + h_ref[m, k]
        for copy in sent:
            copy.wait_send()

    sub = lax.broadcasted_iota(jnp.int32, (SEC_DEV, 128), 0)
    inner = jnp.broadcast_to(lax.rem(owner, SEC_DEV), (SEC_DEV, 128))
    shares = []
    for m in range(members):
        wall = wall_ref[m, 0] * h_ref[m, 0][0:1, :]
        for k in range(1, K):
            wall = wall + wall_ref[m, k] * h_ref[m, k][0:1, :]
        shares.append(jnp.where(sub == inner, jnp.broadcast_to(wall, (SEC_DEV, 128)), 0.0))
    share = jnp.concatenate(shares, axis=0)
    high = share.astype(jnp.bfloat16)
    rest = share - high.astype(jnp.float32)
    middle = rest.astype(jnp.bfloat16)
    low = (rest - middle.astype(jnp.float32)).astype(jnp.bfloat16)
    hot = dest_hot[...]
    sums = lax.dot_general(
        jnp.concatenate([hot, hot, hot], axis=1),
        jnp.concatenate([high, middle, low], axis=1),
        (((1,), (1,)), ((), ())),
        preferred_element_type=jnp.float32,
    )
    width = members * SEC_DEV
    for n in range(n_space):
        sec_tx[n, :, 0:width] = sums[n : n + 1, :]
    for e, peer in enumerate(sec_peers):
        pltpu.make_async_remote_copy(
            src_ref=sec_tx.at[peer[1]], dst_ref=sec_rx.at[e], send_sem=sec_sem.at[0],
            recv_sem=sec_sem.at[1], device_id=peer, device_id_type=MESH,
        ).start()
    write = pltpu.make_async_copy(h_ref, adj_hbm, out_sem)
    write.start()
    every = pltpu.make_async_remote_copy(
        src_ref=sec_tx.at[pl.ds(0, len(sec_peers))], dst_ref=sec_rx, send_sem=sec_sem.at[0],
        recv_sem=sec_sem.at[1], device_id=sec_peers[0], device_id_type=MESH,
    )
    own_share = sec_tx[space]
    every.wait_recv()
    parts = [own_share] + [sec_rx[e] for e in range(len(sec_peers))]
    while len(parts) > 1:
        parts = [parts[n] + parts[n + 1] if n + 1 < len(parts) else parts[n] for n in range(0, len(parts), 2)]
    for m in range(members):
        at = (128 - m * SEC_DEV) % 128
        line = pltpu.roll(parts[0], at, 1) if at else parts[0]
        sens_ref[m : m + 1, :] = line[:, 0:SEC_DEV]
    every.wait_send()
    write.wait()


def on_device(sizes, a, g, d, p, js, jn, jc, colour, wall, owner):
    members, n_inst, n_space, quads = sizes
    field = (members, K, 8, 128)
    flat = (members * K * K * 8, 128)
    vmem, f32 = pltpu.VMEM, jnp.float32
    n_spec, n_sec = n_inst - 1, n_space - 1
    any_spec = pl.BlockSpec(memory_space=pl.ANY)
    adj, sens = pl.pallas_call(
        functools.partial(kernel, sizes),
        out_shape=(jax.ShapeDtypeStruct(field, f32), jax.ShapeDtypeStruct((members, SEC_DEV), f32)),
        in_specs=[any_spec] * 10,
        out_specs=(any_spec, pl.BlockSpec(memory_space=pltpu.VMEM)),
        scratch_shapes=[
            vmem(field, f32), vmem(field, f32), vmem(field, f32),
            vmem((8, 128), jnp.int32), vmem((members, K, 1, 128), f32), vmem((1, 128), jnp.int32),
            vmem((5,) + flat, jnp.bfloat16),
            *[vmem(flat, f32) for _ in range(8)],
            *[vmem(field, f32) for _ in range(4)],
            vmem((PSTEPS, n_spec) + field, f32),
            vmem((2 * PSTEPS, 2) + field, f32),
            vmem((n_space, 128), jnp.bfloat16),
            vmem((n_space, 1, 128), f32),
            vmem((n_sec, 1, 128), f32),
            pltpu.SemaphoreType.DMA((10,)),
            pltpu.SemaphoreType.DMA((PSTEPS, n_spec)),
            pltpu.SemaphoreType.DMA((PSTEPS, n_spec)),
            pltpu.SemaphoreType.DMA((2 * PSTEPS, 2)),
            pltpu.SemaphoreType.DMA((2 * PSTEPS, 2)),
            pltpu.SemaphoreType.DMA((2,)),
            pltpu.SemaphoreType.DMA,
        ],
        compiler_params=pltpu.CompilerParams(
            collective_id=0, has_side_effects=True, vmem_limit_bytes=40 * 1024 * 1024
        ),
        name="adjoint",
    )(
        a.reshape(field), g.reshape(field), *[x.reshape(flat) for x in (d, p, js, jn, jc)],
        colour.reshape(8, 128), wall, owner,
    )
    return adj.reshape(a.shape), sens


def solution(mesh):
    n_inst, n_space = mesh.shape["inst"], mesh.shape["space"]
    sizes = (32 // n_inst, n_inst, n_space, 4)
    return jax.shard_map(
        functools.partial(on_device, sizes),
        mesh=mesh,
        in_specs=(
            P("inst", None, "space", None, None),
            P("inst", None, "space", None, None),
            P("inst", None, None, "space", None, None),
            P("inst", None, None, "space", None, None),
            P("inst", None, None, "space", None, None),
            P("inst", None, None, "space", None, None),
            P("inst", None, None, "space", None, None),
            P("space", None, None),
            P("inst", None, "space", None),
            P("space", None),
        ),
        out_specs=(P("inst", None, "space", None, None), P("inst", "space")),
        check_vma=False,
    )
```

```python
import functools
import math

import jax
import jax.numpy as jnp
from jax import lax
from jax.experimental import pallas as pl
from jax.experimental.pallas import tpu as pltpu
from jax.sharding import PartitionSpec as P

NCOL = 4
PSTEPS = 2
SEC_DEV = 8
GAIN = 0.25
K = 5
GATHER, SCATTER = (0, 1), (2, 3, 4)
MESH = pl.DeviceIdType.MESH


def spectral_row(count):
    row = [0.0]
    for gap in range(1, count):
        sign = 1.0 if gap % 2 == 0 else -1.0
        row.append(GAIN * 0.5 * sign / math.tan(math.pi * gap / count))
    return row


def ring_order(count):
    half = count // 2
    order = [half]
    for step in range(1, half + 1):
        for offset in (half - step, half + step):
            if 0 <= offset < count:
                order.append(offset)
    return order


def kernel(
    sizes,
    a_hbm, g_hbm, d_hbm, p_hbm, js_hbm, jn_hbm, jc_hbm, col_hbm, wall_hbm, own_hbm,
    adj_ref, sens_ref,
    a_ref, a1_ref, g_ref, col_ref, wall_ref, own_ref, raw,
    dm, pm, jsm, jnm, jcm, ps, pn, pc,
    rs, b_ref, u_ref, h_ref, ya_rx, xa_tx, xa_rx, xb_rx, yb_tx, yb_rx, halo_rx, dest_hot, sec_tx, sec_rx,
    in_sem, ya_sem, xa_sem, xb_sem, yb_sem, halo_tx_sem, halo_rx_sem, sec_sem, known_sem,
):
    members, n_inst, n_space, quads = sizes
    row = spectral_row(members * n_inst)
    inst = lax.axis_index("inst")
    space = lax.axis_index("space")

    side = n_inst // 2
    high, why = inst // side, lax.rem(inst, side)
    y_peers = [(high * side + lax.rem(why + d, side), space) for d in range(1, side)]
    x_peer = (lax.rem(inst + side, n_inst), space)
    halo_peers = [(inst, lax.rem(space + 1, n_space)), (inst, lax.rem(space + n_space - 1, n_space))]
    rings = n_space // quads
    zed, quad = space // quads, lax.rem(space, quads)
    sec_peers = []
    for dz in ring_order(rings):
        for dq in range(quads):
            if dz or dq:
                sec_peers.append((inst, lax.rem(zed + dz, rings) * quads + lax.rem(quad + dq, quads)))

    barrier = pltpu.get_barrier_semaphore()
    near = y_peers + [x_peer] + halo_peers
    for peer in near:
        pl.semaphore_signal(barrier, inc=1, device_id=peer, device_id_type=MESH)
    loads = [
        pltpu.make_async_copy(src, dst, in_sem.at[n])
        for n, (src, dst) in enumerate(
            [
                (a_hbm, a_ref), (g_hbm, g_ref), (col_hbm, col_ref), (wall_hbm, wall_ref), (own_hbm, own_ref),
                (p_hbm, raw.at[0]), (jn_hbm, raw.at[1]), (jc_hbm, raw.at[2]), (js_hbm, raw.at[3]), (d_hbm, raw.at[4]),
            ]
        )
    ]
    for load in loads:
        load.start()
    for load in loads:
        load.wait()
    rows = members * K * K * 8
    part = 160
    for n, wide in enumerate((pm, jnm, jcm, jsm, dm)):
        @pl.loop(0, rows // part)
        def _(i, n=n, wide=wide):
            at = pl.multiple_of(i * part, part)
            wide[pl.ds(at, part), :] = raw[n, pl.ds(at, part), :].astype(jnp.float32)

    pl.semaphore_wait(barrier, len(near))

    def remote(source, target, sems, index, peer):
        copy = pltpu.make_async_remote_copy(
            src_ref=source, dst_ref=target, send_sem=sems.at[(0,) + index], recv_sem=sems.at[(1,) + index],
            device_id=peer, device_id_type=MESH,
        )
        copy.start()
        return copy

    def weight(offset, moved):
        one, two = row[offset % len(row)], row[(offset + len(row) // 2) % len(row)]
        return jnp.where(moved, jnp.float32(two), jnp.float32(one))

    spread = range(1 - members, members)
    from_weight, from_pair, to_weight, to_pair = {}, {}, {}, {}
    for d in range(1, side):
        for gap in spread:
            offset = gap - members * d
            half = len(row) // 2
            from_weight[d, gap] = weight(offset, why < d)
            from_pair[d, gap] = weight(offset + half, why < d)
            to_weight[d, gap] = weight(offset, why >= side - d)
            to_pair[d, gap] = weight(offset + half, why >= side - d)

    def near_sum(v, m, shift, total=None):
        for j in range(members):
            entry = row[(j - m + shift) % len(row)]
            if entry:
                total = entry * v[j] if total is None else total + entry * v[j]
        return total

    def spectral_start(step, source):
        copies = {}
        for k in SCATTER:
            copies["xb", k] = remote(source.at[:, k], xb_rx.at[step, k], xb_sem, (step, k), x_peer)
        for k in GATHER:
            for d, peer in enumerate(y_peers):
                copies["ya", k, d] = remote(source.at[:, k], ya_rx.at[step, d, k], ya_sem, (step, d, k), peer)
        return copies

    def spectral_own(source):
        for k in range(K):
            v = [source[j, k] for j in range(members)]
            for m in range(members):
                rs[m, k] = rs[m, k] - near_sum(v, m, 0)

    def spectral_middle(step, source, copies):
        half = len(row) // 2
        for k in SCATTER:
            v = [source[j, k] for j in range(members)]
            copies["xb", k].wait_recv()
            w = [xb_rx[step, k, j] for j in range(members)]
            for d in range(1, side):
                for m in range(members):
                    total = to_weight[d, -m] * v[0] + to_pair[d, -m] * w[0]
                    for j in range(1, members):
                        total = total + (to_weight[d, j - m] * v[j] + to_pair[d, j - m] * w[j])
                    yb_tx[step, d - 1, k, m] = total
                copies["yb", k, d - 1] = remote(
                    yb_tx.at[step, d - 1, k], yb_rx.at[step, d - 1, k], yb_sem, (step, d - 1, k), y_peers[d - 1]
                )
            for m in range(members):
                rs[m, k] = rs[m, k] - near_sum(w, m, half)
        for k in GATHER:
            for d in range(side - 1):
                copies["ya", k, d].wait_recv()
            v = [source[j, k] for j in range(members)]
            others = [[ya_rx[step, d, k, j] for j in range(members)] for d in range(side - 1)]
            for m in range(members):
                total = near_sum(v, m, half)
                for d in range(1, side):
                    for j in range(members):
                        total = total + from_pair[d, j - m] * others[d - 1][j]
                xa_tx[step, k, m] = total
            copies["xa", k] = remote(xa_tx.at[step, k], xa_rx.at[step, k], xa_sem, (step, k), x_peer)
            for m in range(members):
                total = rs[m, k]
                for d in range(1, side):
                    for j in range(members):
                        total = total - from_weight[d, j - m] * others[d - 1][j]
                rs[m, k] = total

    def spectral_end(step, copies):
        for k in GATHER:
            copies["xa", k].wait_recv()
            for m in range(members):
                rs[m, k] = rs[m, k] - xa_rx[step, k, m]
        for k in SCATTER:
            for d in range(side - 1):
                copies["yb", k, d].wait_recv()
            for m in range(members):
                rs[m, k] = rs[m, k] - (yb_rx[step, 0, k, m] + yb_rx[step, 1, k, m] + yb_rx[step, 2, k, m])

    def tell(turn):
        for far in (1 << turn, n_space - (1 << turn)):
            pl.semaphore_signal(
                known_sem.at[turn], inc=1, device_id=(inst, lax.rem(space + far, n_space)), device_id_type=MESH
            )

    def learn(turn):
        pl.semaphore_wait(known_sem.at[turn], 2)

    def send_halo(slot, source):
        halo = []
        for side, peer in enumerate(halo_peers):
            copy = pltpu.make_async_remote_copy(
                src_ref=source, dst_ref=halo_rx.at[slot, side], send_sem=halo_tx_sem.at[slot, side],
                recv_sem=halo_rx_sem.at[slot, side], device_id=peer, device_id_type=MESH,
            )
            copy.start()
            halo.append(copy)
        return halo

    def block(ref, m, k, l):
        at = (m * K * K + k * K + l) * 8
        if not isinstance(at, int):
            at = pl.multiple_of(at, 8)
        return ref[pl.ds(at, 8), :]

    lane_row = lax.broadcasted_iota(jnp.int32, (8, 128), 0)

    def normal_diff(v):
        minus = jnp.where(lane_row > 0, pltpu.roll(v, 1, 0), 0.0)
        plus = jnp.where(lane_row < 7, pltpu.roll(v, 7, 0), 0.0)
        return minus - plus

    def chord_diff(v):
        return pltpu.roll(v, 1, 1) - pltpu.roll(v, 127, 1)

    def span_diff(slot, m, l):
        minus = jnp.where(space > 0, halo_rx[slot, 0, m, l], 0.0)
        plus = jnp.where(space < n_space - 1, halo_rx[slot, 1, m, l], 0.0)
        return minus - plus

    def fold():
        @pl.loop(0, members)
        def _(m):
            for jac, product in ((jnm, pn), (jcm, pc), (jsm, ps)):
                right = [[0.5 * block(jac, m, j, l) for l in range(K)] for j in range(K)]
                for k in range(K):
                    left = [block(pm, m, k, j) for j in range(K)]
                    for l in range(K):
                        total = left[0] * right[0][l]
                        for j in range(1, K):
                            total = total + left[j] * right[j][l]
                        at = pl.multiple_of((m * K * K + k * K + l) * 8, 8)
                        product[pl.ds(at, 8), :] = total

    state = a_ref
    spec = spectral_start(0, state)
    halo_a = send_halo(0, state)
    tell(0)

    owner = own_ref[...]
    dest_hot[...] = jnp.where(
        lax.broadcasted_iota(jnp.int32, (n_space, 128), 0) == jnp.broadcast_to(owner // SEC_DEV, (n_space, 128)), 1.0, 0.0
    ).astype(jnp.bfloat16)
    sec_tx[...] = jnp.zeros_like(sec_tx)
    colour = col_ref[...]

    for step in range(PSTEPS):
        @pl.loop(0, members)
        def _(m, state=state):
            v = [state[m, l] for l in range(K)]
            dn = [normal_diff(v[l]) for l in range(K)]
            dc = [chord_diff(v[l]) for l in range(K)]
            for k in range(K):
                local = block(dm, m, k, 0) * v[0]
                cross = block(jnm, m, k, 0) * dn[0] + block(jcm, m, k, 0) * dc[0]
                for l in range(1, K):
                    local = local + block(dm, m, k, l) * v[l]
                    cross = cross + (block(jnm, m, k, l) * dn[l] + block(jcm, m, k, l) * dc[l])
                rs[m, k] = g_ref[m, k] - (local + 0.5 * cross)

        spectral_own(state)
        spectral_middle(step, state, spec)
        if step == 0:
            fold()
        for copy in halo_a:
            copy.wait_recv()

        @pl.loop(0, members)
        def _(m, step=step):
            ds = [span_diff(2 * step, m, l) for l in range(K)]
            for k in range(K):
                cross = block(jsm, m, k, 0) * ds[0]
                for l in range(1, K):
                    cross = cross + block(jsm, m, k, l) * ds[l]
                rs[m, k] = rs[m, k] - 0.5 * cross

        learn(3 * step)
        tell(3 * step + 1)
        spectral_end(step, spec)

        for m in range(members):
            r = [rs[m, l] for l in range(K)]
            for k in range(K):
                total = block(pm, m, k, 0) * r[0]
                for l in range(1, K):
                    total = total + block(pm, m, k, l) * r[l]
                b_ref[m, k] = total
                u_ref[m, k] = jnp.where(colour == 0, total, 0.0)

        def cross_terms(m, source):
            v = [source[m, l] for l in range(K)]
            dn = [normal_diff(v[l]) for l in range(K)]
            dc = [chord_diff(v[l]) for l in range(K)]
            out = []
            for k in range(K):
                total = block(pn, m, k, 0) * dn[0] + block(pc, m, k, 0) * dc[0]
                for l in range(1, K):
                    total = total + (block(pn, m, k, l) * dn[l] + block(pc, m, k, l) * dc[l])
                out.append(total)
            return v, out

        @pl.loop(1, NCOL)
        def _(value):
            mine = colour == value
            for m in range(members):
                v, cross = cross_terms(m, u_ref)
                for k in range(K):
                    u_ref[m, k] = jnp.where(mine, b_ref[m, k] - cross[k], v[k])

        halo_u = send_halo(2 * step + 1, u_ref)
        for m in range(members):
            _, cross = cross_terms(m, u_ref)
            for k in range(K):
                rs[m, k] = cross[k]
        if step == 0:
            learn(1)
            tell(2)
        for copy in halo_u:
            copy.wait_recv()
        for m in range(members):
            ds = [span_diff(2 * step + 1, m, l) for l in range(K)]
            for k in range(K):
                total = b_ref[m, k]
                for l in range(K):
                    total = total - block(ps, m, k, l) * ds[l]
                b_ref[m, k] = total
                h_ref[m, k] = jnp.where(colour == NCOL - 1, total - rs[m, k], u_ref[m, k])

        @pl.loop(1, NCOL)
        def _(back):
            mine = colour == NCOL - 1 - back
            for m in range(members):
                v, cross = cross_terms(m, h_ref)
                for k in range(K):
                    h_ref[m, k] = jnp.where(mine, b_ref[m, k] - cross[k], v[k])

        sent = list(spec.values()) + halo_a + halo_u
        if step < PSTEPS - 1:
            for m in range(members):
                for k in range(K):
                    a1_ref[m, k] = state[m, k] + h_ref[m, k]
            spec = spectral_start(step + 1, a1_ref)
            halo_a = send_halo(2 * step + 2, a1_ref)
            state = a1_ref
            learn(2)
            tell(3)
        else:
            for m in range(members):
                for k in range(K):
                    adj_ref[m, k] = state[m, k] + h_ref[m, k]
        for copy in sent:
            copy.wait_send()

    sub = lax.broadcasted_iota(jnp.int32, (SEC_DEV, 128), 0)
    inner = jnp.broadcast_to(lax.rem(owner, SEC_DEV), (SEC_DEV, 128))
    shares = []
    for m in range(members):
        wall = wall_ref[m, 0] * adj_ref[m, 0][0:1, :]
        for k in range(1, K):
            wall = wall + wall_ref[m, k] * adj_ref[m, k][0:1, :]
        shares.append(jnp.where(sub == inner, jnp.broadcast_to(wall, (SEC_DEV, 128)), 0.0))
    share = jnp.concatenate(shares, axis=0)
    high = share.astype(jnp.bfloat16)
    rest = share - high.astype(jnp.float32)
    middle = rest.astype(jnp.bfloat16)
    low = (rest - middle.astype(jnp.float32)).astype(jnp.bfloat16)
    hot = dest_hot[...]
    sums = lax.dot_general(
        jnp.concatenate([hot, hot, hot], axis=1),
        jnp.concatenate([high, middle, low], axis=1),
        (((1,), (1,)), ((), ())),
        preferred_element_type=jnp.float32,
    )
    width = members * SEC_DEV
    for n in range(n_space):
        sec_tx[n, :, 0:width] = sums[n : n + 1, :]
    learn(4)
    for e, peer in enumerate(sec_peers):
        pltpu.make_async_remote_copy(
            src_ref=sec_tx.at[peer[1]], dst_ref=sec_rx.at[e], send_sem=sec_sem.at[0],
            recv_sem=sec_sem.at[1], device_id=peer, device_id_type=MESH,
        ).start()
    every = pltpu.make_async_remote_copy(
        src_ref=sec_tx.at[pl.ds(0, len(sec_peers))], dst_ref=sec_rx, send_sem=sec_sem.at[0],
        recv_sem=sec_sem.at[1], device_id=sec_peers[0], device_id_type=MESH,
    )
    own_share = sec_tx[space]
    every.wait_recv()
    parts = [own_share] + [sec_rx[e] for e in range(len(sec_peers))]
    while len(parts) > 1:
        parts = [parts[n] + parts[n + 1] if n + 1 < len(parts) else parts[n] for n in range(0, len(parts), 2)]
    for m in range(members):
        at = (128 - m * SEC_DEV) % 128
        line = pltpu.roll(parts[0], at, 1) if at else parts[0]
        sens_ref[m : m + 1, :] = line[:, 0:SEC_DEV]
    every.wait_send()


def on_device(sizes, a, g, d, p, js, jn, jc, colour, wall, owner):
    members, n_inst, n_space, quads = sizes
    field = (members, K, 8, 128)
    flat = (members * K * K * 8, 128)
    vmem, f32 = pltpu.VMEM, jnp.float32
    lump, side, n_sec = (members, 8, 128), n_inst // 2, n_space - 1
    hbm_spec = pl.BlockSpec(memory_space=pltpu.HBM)
    adj, sens = pl.pallas_call(
        functools.partial(kernel, sizes),
        out_shape=(vmem(field, f32), vmem((members, SEC_DEV), f32)),
        in_specs=[hbm_spec] * 10,
        out_specs=(pl.BlockSpec(memory_space=pltpu.VMEM), pl.BlockSpec(memory_space=pltpu.VMEM)),
        scratch_shapes=[
            vmem(field, f32), vmem(field, f32), vmem(field, f32),
            vmem((8, 128), jnp.int32), vmem((members, K, 1, 128), f32), vmem((1, 128), jnp.int32),
            vmem((5,) + flat, jnp.bfloat16),
            *[vmem(flat, f32) for _ in range(8)],
            *[vmem(field, f32) for _ in range(4)],
            vmem((PSTEPS, side - 1, K) + lump, f32),
            *[vmem((PSTEPS, K) + lump, f32) for _ in range(3)],
            *[vmem((PSTEPS, side - 1, K) + lump, f32) for _ in range(2)],
            vmem((2 * PSTEPS, 2) + field, f32),
            vmem((n_space, 128), jnp.bfloat16),
            vmem((n_space, 1, 128), f32),
            vmem((n_sec, 1, 128), f32),
            pltpu.SemaphoreType.DMA((10,)),
            pltpu.SemaphoreType.DMA((2, PSTEPS, side - 1, K)),
            pltpu.SemaphoreType.DMA((2, PSTEPS, K)),
            pltpu.SemaphoreType.DMA((2, PSTEPS, K)),
            pltpu.SemaphoreType.DMA((2, PSTEPS, side - 1, K)),
            pltpu.SemaphoreType.DMA((2 * PSTEPS, 2)),
            pltpu.SemaphoreType.DMA((2 * PSTEPS, 2)),
            pltpu.SemaphoreType.DMA((2,)),
            pltpu.SemaphoreType.REGULAR((5,)),
        ],
        compiler_params=pltpu.CompilerParams(
            collective_id=0, has_side_effects=True, vmem_limit_bytes=60 * 1024 * 1024
        ),
        name="adjoint",
    )(
        a.reshape(field), g.reshape(field), *[x.reshape(flat) for x in (d, p, js, jn, jc)],
        colour.reshape(8, 128), wall, owner,
    )
    return adj.reshape(a.shape), sens


def solution(mesh):
    n_inst, n_space = mesh.shape["inst"], mesh.shape["space"]
    sizes = (32 // n_inst, n_inst, n_space, 4)
    return jax.shard_map(
        functools.partial(on_device, sizes),
        mesh=mesh,
        in_specs=(
            P("inst", None, "space", None, None),
            P("inst", None, "space", None, None),
            P("inst", None, None, "space", None, None),
            P("inst", None, None, "space", None, None),
            P("inst", None, None, "space", None, None),
            P("inst", None, None, "space", None, None),
            P("inst", None, None, "space", None, None),
            P("space", None, None),
            P("inst", None, "space", None),
            P("space", None),
        ),
        out_specs=(P("inst", None, "space", None, None), P("inst", "space")),
        check_vma=False,
    )
```

```python
import functools
import math

import jax
import jax.numpy as jnp
from jax import lax
from jax.experimental import pallas as pl
from jax.experimental.pallas import tpu as pltpu
from jax.sharding import PartitionSpec as P

NCOL = 4
PSTEPS = 2
SEC_DEV = 8
GAIN = 0.25
K = 5
GATHER, SCATTER = (0, 1), (2, 3, 4)
FAR, MATE = 0, 1
MESH = pl.DeviceIdType.MESH


def spectral_row(count):
    row = [0.0]
    for gap in range(1, count):
        sign = 1.0 if gap % 2 == 0 else -1.0
        row.append(GAIN * 0.5 * sign / math.tan(math.pi * gap / count))
    return row


def ring_order(count):
    half = count // 2
    order = [half]
    for step in range(1, half + 1):
        for offset in (half - step, half + step):
            if 0 <= offset < count:
                order.append(offset)
    return order


def kernel(
    sizes,
    a_hbm, g_hbm, d_hbm, p_hbm, js_hbm, jn_hbm, jc_hbm, col_hbm, wall_hbm, own_hbm,
    adj_ref, sens_ref,
    a_ref, a1_ref, g_ref, col_ref, wall_ref, own_ref, raw,
    dm, pm, jsm, jnm, jcm, ps, pn, pc,
    rs, b_ref, u_ref, h_ref, ya_rx, xa_tx, xa_rx, xb_rx, yb_tx, yb_rx, halo_rx, dest_hot, sec_tx, sec_rx,
    in_sem, ya_sem, xa_sem, xb_sem, yb_sem, halo_sem, sec_sem, known_sem,
):
    members, n_inst, n_space, quads = sizes
    row = spectral_row(members * n_inst)
    inst = lax.axis_index("inst")
    space = lax.axis_index("space")

    side = n_inst // 2
    high, why = inst // side, lax.rem(inst, side)
    y_peers = [(high * side + lax.rem(why + d, side), space) for d in range(1, side)]
    x_peer = (lax.rem(inst + side, n_inst), space)
    even = lax.rem(space, 2) == 0
    far = space + jnp.where(even, n_space - 1, 1)
    halo_peers = {FAR: (inst, lax.rem(far, n_space)), MATE: (inst, space + jnp.where(even, 1, -1))}
    far_there = jnp.logical_and(space > 0, space < n_space - 1)
    rings = n_space // quads
    zed, quad = space // quads, lax.rem(space, quads)
    sec_peers = []
    for dz in ring_order(rings):
        for dq in range(quads):
            if dz or dq:
                sec_peers.append((inst, lax.rem(zed + dz, rings) * quads + lax.rem(quad + dq, quads)))

    barrier = pltpu.get_barrier_semaphore()
    near = y_peers + [x_peer] + [halo_peers[FAR], halo_peers[MATE]]
    for peer in near:
        pl.semaphore_signal(barrier, inc=1, device_id=peer, device_id_type=MESH)
    loads = [
        pltpu.make_async_copy(src, dst, in_sem.at[n])
        for n, (src, dst) in enumerate(
            [
                (a_hbm, a_ref), (g_hbm, g_ref), (col_hbm, col_ref), (wall_hbm, wall_ref), (own_hbm, own_ref),
                (p_hbm, raw.at[0]), (jn_hbm, raw.at[1]), (jc_hbm, raw.at[2]), (js_hbm, raw.at[3]), (d_hbm, raw.at[4]),
            ]
        )
    ]
    for load in loads:
        load.start()
    for load in loads:
        load.wait()
    rows = members * K * K * 8
    part = 160
    for n, wide in enumerate((pm, jnm, jcm, jsm, dm)):
        @pl.loop(0, rows // part)
        def _(i, n=n, wide=wide):
            at = pl.multiple_of(i * part, part)
            wide[pl.ds(at, part), :] = raw[n, pl.ds(at, part), :].astype(jnp.float32)

    pl.semaphore_wait(barrier, len(near))

    def remote(source, target, sems, index, peer):
        copy = pltpu.make_async_remote_copy(
            src_ref=source, dst_ref=target, send_sem=sems.at[(0,) + index], recv_sem=sems.at[(1,) + index],
            device_id=peer, device_id_type=MESH,
        )
        copy.start()
        return copy

    def weight(offset, moved):
        one, two = row[offset % len(row)], row[(offset + len(row) // 2) % len(row)]
        return jnp.where(moved, jnp.float32(two), jnp.float32(one))

    spread = range(1 - members, members)
    from_weight, from_pair, to_weight, to_pair = {}, {}, {}, {}
    for d in range(1, side):
        for gap in spread:
            offset = gap - members * d
            half = len(row) // 2
            from_weight[d, gap] = weight(offset, why < d)
            from_pair[d, gap] = weight(offset + half, why < d)
            to_weight[d, gap] = weight(offset, why >= side - d)
            to_pair[d, gap] = weight(offset + half, why >= side - d)

    def near_sum(v, m, shift, total=None):
        for j in range(members):
            entry = row[(j - m + shift) % len(row)]
            if entry:
                total = entry * v[j] if total is None else total + entry * v[j]
        return total

    def spectral_start(step, source):
        copies = {}
        for k in SCATTER:
            copies["xb", k] = remote(source.at[:, k], xb_rx.at[step, k], xb_sem, (step, k), x_peer)
        for k in GATHER:
            for d, peer in enumerate(y_peers):
                copies["ya", k, d] = remote(source.at[:, k], ya_rx.at[step, d, k], ya_sem, (step, d, k), peer)
        return copies

    def spectral_own(source):
        for k in range(K):
            v = [source[j, k] for j in range(members)]
            for m in range(members):
                rs[m, k] = rs[m, k] - near_sum(v, m, 0)

    def spectral_middle(step, source, copies):
        half = len(row) // 2
        for k in SCATTER:
            v = [source[j, k] for j in range(members)]
            copies["xb", k].wait_recv()
            w = [xb_rx[step, k, j] for j in range(members)]
            for d in range(1, side):
                for m in range(members):
                    total = to_weight[d, -m] * v[0] + to_pair[d, -m] * w[0]
                    for j in range(1, members):
                        total = total + (to_weight[d, j - m] * v[j] + to_pair[d, j - m] * w[j])
                    yb_tx[step, d - 1, k, m] = total
                copies["yb", k, d - 1] = remote(
                    yb_tx.at[step, d - 1, k], yb_rx.at[step, d - 1, k], yb_sem, (step, d - 1, k), y_peers[d - 1]
                )
            for m in range(members):
                rs[m, k] = rs[m, k] - near_sum(w, m, half)
        for k in GATHER:
            for d in range(side - 1):
                copies["ya", k, d].wait_recv()
            v = [source[j, k] for j in range(members)]
            others = [[ya_rx[step, d, k, j] for j in range(members)] for d in range(side - 1)]
            for m in range(members):
                total = near_sum(v, m, half)
                for d in range(1, side):
                    for j in range(members):
                        total = total + from_pair[d, j - m] * others[d - 1][j]
                xa_tx[step, k, m] = total
            copies["xa", k] = remote(xa_tx.at[step, k], xa_rx.at[step, k], xa_sem, (step, k), x_peer)
            for m in range(members):
                total = rs[m, k]
                for d in range(1, side):
                    for j in range(members):
                        total = total - from_weight[d, j - m] * others[d - 1][j]
                rs[m, k] = total

    def spectral_end(step, copies):
        for k in GATHER:
            copies["xa", k].wait_recv()
            for m in range(members):
                rs[m, k] = rs[m, k] - xa_rx[step, k, m]
        for k in SCATTER:
            for d in range(side - 1):
                copies["yb", k, d].wait_recv()
            for m in range(members):
                rs[m, k] = rs[m, k] - (yb_rx[step, 0, k, m] + yb_rx[step, 1, k, m] + yb_rx[step, 2, k, m])

    def tell(turn):
        for far in (1 << turn, n_space - (1 << turn)):
            pl.semaphore_signal(
                known_sem.at[turn], inc=1, device_id=(inst, lax.rem(space + far, n_space)), device_id_type=MESH
            )

    def learn(turn):
        pl.semaphore_wait(known_sem.at[turn], 2)

    def send_halo(slot, source, part=None):
        some = pl.ds(0, members) if part is None else pl.ds(part * (members // 2), members // 2)
        copies = []
        for which in (FAR, MATE):
            copy = pltpu.make_async_remote_copy(
                src_ref=source.at[some], dst_ref=halo_rx.at[slot, which, some],
                send_sem=halo_sem.at[0, slot, which, part or 0], recv_sem=halo_sem.at[1, slot, which, part or 0],
                device_id=halo_peers[which], device_id_type=MESH,
            )
            copy.start()
            copies.append(copy)
        return copies

    def block(ref, m, k, l):
        at = (m * K * K + k * K + l) * 8
        if not isinstance(at, int):
            at = pl.multiple_of(at, 8)
        return ref[pl.ds(at, 8), :]

    lane_row = lax.broadcasted_iota(jnp.int32, (8, 128), 0)

    def normal_diff(v):
        minus = jnp.where(lane_row > 0, pltpu.roll(v, 1, 0), 0.0)
        plus = jnp.where(lane_row < 7, pltpu.roll(v, 7, 0), 0.0)
        return minus - plus

    def chord_diff(v):
        return pltpu.roll(v, 1, 1) - pltpu.roll(v, 127, 1)

    def span_diff(slot, m, l):
        far = jnp.where(far_there, halo_rx[slot, FAR, m, l], 0.0)
        mate = halo_rx[slot, MATE, m, l]
        return jnp.where(even, far - mate, mate - far)

    def fold():
        @pl.loop(0, members)
        def _(m):
            for jac, product in ((jnm, pn), (jcm, pc), (jsm, ps)):
                right = [[0.5 * block(jac, m, j, l) for l in range(K)] for j in range(K)]
                for k in range(K):
                    left = [block(pm, m, k, j) for j in range(K)]
                    for l in range(K):
                        total = left[0] * right[0][l]
                        for j in range(1, K):
                            total = total + left[j] * right[j][l]
                        at = pl.multiple_of((m * K * K + k * K + l) * 8, 8)
                        product[pl.ds(at, 8), :] = total

    state = a_ref
    spec = spectral_start(0, state)
    halo_a = send_halo(0, state)
    tell(0)

    owner = own_ref[...]
    dest_hot[...] = jnp.where(
        lax.broadcasted_iota(jnp.int32, (n_space, 128), 0) == jnp.broadcast_to(owner // SEC_DEV, (n_space, 128)), 1.0, 0.0
    ).astype(jnp.bfloat16)
    sec_tx[...] = jnp.zeros_like(sec_tx)
    colour = col_ref[...]

    for step in range(PSTEPS):
        @pl.loop(0, members)
        def _(m, state=state):
            v = [state[m, l] for l in range(K)]
            dn = [normal_diff(v[l]) for l in range(K)]
            dc = [chord_diff(v[l]) for l in range(K)]
            for k in range(K):
                local = block(dm, m, k, 0) * v[0]
                cross = block(jnm, m, k, 0) * dn[0] + block(jcm, m, k, 0) * dc[0]
                for l in range(1, K):
                    local = local + block(dm, m, k, l) * v[l]
                    cross = cross + (block(jnm, m, k, l) * dn[l] + block(jcm, m, k, l) * dc[l])
                rs[m, k] = g_ref[m, k] - (local + 0.5 * cross)

        spectral_own(state)
        spectral_middle(step, state, spec)
        if step == 0:
            fold()
        for copy in halo_a:
            copy.wait_recv()

        @pl.loop(0, members)
        def _(m, step=step):
            ds = [span_diff(2 * step, m, l) for l in range(K)]
            for k in range(K):
                cross = block(jsm, m, k, 0) * ds[0]
                for l in range(1, K):
                    cross = cross + block(jsm, m, k, l) * ds[l]
                rs[m, k] = rs[m, k] - 0.5 * cross

        learn(3 * step)
        tell(3 * step + 1)
        spectral_end(step, spec)

        def cross_terms(m, source):
            v = [source[m, l] for l in range(K)]
            dn = [normal_diff(v[l]) for l in range(K)]
            dc = [chord_diff(v[l]) for l in range(K)]
            out = []
            for k in range(K):
                total = block(pn, m, k, 0) * dn[0] + block(pc, m, k, 0) * dc[0]
                for l in range(1, K):
                    total = total + (block(pn, m, k, l) * dn[l] + block(pc, m, k, l) * dc[l])
                out.append(total)
            return v, out

        def visit(mine, some, field):
            for m in some:
                v, cross = cross_terms(m, field)
                for k in range(K):
                    field[m, k] = jnp.where(mine, b_ref[m, k] - cross[k], v[k])

        halves = [range(members // 2), range(members // 2, members)]

        halo_u = []
        for part, some in enumerate(halves):
            for m in some:
                r = [rs[m, l] for l in range(K)]
                for k in range(K):
                    total = block(pm, m, k, 0) * r[0]
                    for l in range(1, K):
                        total = total + block(pm, m, k, l) * r[l]
                    b_ref[m, k] = total
                    u_ref[m, k] = jnp.where(colour == 0, total, 0.0)

            @pl.loop(1, NCOL)
            def _(value, some=some):
                visit(colour == value, some, u_ref)

            halo_u.append(send_halo(2 * step + 1, u_ref, part))

        for m in range(members):
            _, cross = cross_terms(m, u_ref)
            for k in range(K):
                rs[m, k] = cross[k]
        if step == 0:
            learn(1)
            tell(2)
        for part, some in enumerate(halves):
            for copy in halo_u[part]:
                copy.wait_recv()
            for m in some:
                ds = [span_diff(2 * step + 1, m, l) for l in range(K)]
                for k in range(K):
                    total = b_ref[m, k]
                    for l in range(K):
                        total = total - block(ps, m, k, l) * ds[l]
                    b_ref[m, k] = total
                    h_ref[m, k] = jnp.where(colour == NCOL - 1, total - rs[m, k], u_ref[m, k])

            @pl.loop(1, NCOL)
            def _(back, some=some):
                visit(colour == NCOL - 1 - back, some, h_ref)

        sent = list(spec.values()) + halo_a + halo_u[0] + halo_u[1]
        if step < PSTEPS - 1:
            for m in range(members):
                for k in range(K):
                    a1_ref[m, k] = state[m, k] + h_ref[m, k]
            spec = spectral_start(step + 1, a1_ref)
            halo_a = send_halo(2 * step + 2, a1_ref)
            state = a1_ref
            learn(2)
            tell(3)
        else:
            for m in range(members):
                for k in range(K):
                    adj_ref[m, k] = state[m, k] + h_ref[m, k]
        for copy in sent:
            copy.wait_send()

    sub = lax.broadcasted_iota(jnp.int32, (SEC_DEV, 128), 0)
    inner = jnp.broadcast_to(lax.rem(owner, SEC_DEV), (SEC_DEV, 128))
    shares = []
    for m in range(members):
        wall = wall_ref[m, 0] * adj_ref[m, 0][0:1, :]
        for k in range(1, K):
            wall = wall + wall_ref[m, k] * adj_ref[m, k][0:1, :]
        shares.append(jnp.where(sub == inner, jnp.broadcast_to(wall, (SEC_DEV, 128)), 0.0))
    share = jnp.concatenate(shares, axis=0)
    high = share.astype(jnp.bfloat16)
    rest = share - high.astype(jnp.float32)
    middle = rest.astype(jnp.bfloat16)
    low = (rest - middle.astype(jnp.float32)).astype(jnp.bfloat16)
    hot = dest_hot[...]
    sums = lax.dot_general(
        jnp.concatenate([hot, hot, hot], axis=1),
        jnp.concatenate([high, middle, low], axis=1),
        (((1,), (1,)), ((), ())),
        preferred_element_type=jnp.float32,
    )
    width = members * SEC_DEV
    for n in range(n_space):
        sec_tx[n, :, 0:width] = sums[n : n + 1, :]
    learn(4)
    for e, peer in enumerate(sec_peers):
        pltpu.make_async_remote_copy(
            src_ref=sec_tx.at[peer[1]], dst_ref=sec_rx.at[e], send_sem=sec_sem.at[0],
            recv_sem=sec_sem.at[1], device_id=peer, device_id_type=MESH,
        ).start()
    every = pltpu.make_async_remote_copy(
        src_ref=sec_tx.at[pl.ds(0, len(sec_peers))], dst_ref=sec_rx, send_sem=sec_sem.at[0],
        recv_sem=sec_sem.at[1], device_id=sec_peers[0], device_id_type=MESH,
    )
    own_share = sec_tx[space]
    every.wait_recv()
    parts = [own_share] + [sec_rx[e] for e in range(len(sec_peers))]
    while len(parts) > 1:
        parts = [parts[n] + parts[n + 1] if n + 1 < len(parts) else parts[n] for n in range(0, len(parts), 2)]
    for m in range(members):
        at = (128 - m * SEC_DEV) % 128
        line = pltpu.roll(parts[0], at, 1) if at else parts[0]
        sens_ref[m : m + 1, :] = line[:, 0:SEC_DEV]
    every.wait_send()


def finish(adj_ref, sens_ref, adj_out, sens_out, sem):
    one = pltpu.make_async_copy(adj_ref, adj_out, sem.at[0])
    two = pltpu.make_async_copy(sens_ref, sens_out, sem.at[1])
    one.start()
    two.start()
    one.wait()
    two.wait()


def on_device(sizes, a, g, d, p, js, jn, jc, colour, wall, owner):
    members, n_inst, n_space, quads = sizes
    field = (members, K, 8, 128)
    flat = (members * K * K * 8, 128)
    vmem, f32 = pltpu.VMEM, jnp.float32
    lump, side, n_sec = (members, 8, 128), n_inst // 2, n_space - 1
    hbm_spec = pl.BlockSpec(memory_space=pltpu.HBM)
    adj, sens = pl.pallas_call(
        functools.partial(kernel, sizes),
        out_shape=(vmem(field, f32), vmem((members, SEC_DEV), f32)),
        in_specs=[hbm_spec] * 10,
        out_specs=(pl.BlockSpec(memory_space=pltpu.VMEM), pl.BlockSpec(memory_space=pltpu.VMEM)),
        scratch_shapes=[
            vmem(field, f32), vmem(field, f32), vmem(field, f32),
            vmem((8, 128), jnp.int32), vmem((members, K, 1, 128), f32), vmem((1, 128), jnp.int32),
            vmem((5,) + flat, jnp.bfloat16),
            *[vmem(flat, f32) for _ in range(8)],
            *[vmem(field, f32) for _ in range(4)],
            vmem((PSTEPS, side - 1, K) + lump, f32),
            *[vmem((PSTEPS, K) + lump, f32) for _ in range(3)],
            *[vmem((PSTEPS, side - 1, K) + lump, f32) for _ in range(2)],
            vmem((2 * PSTEPS, 2) + field, f32),
            vmem((n_space, 128), jnp.bfloat16),
            vmem((n_space, 1, 128), f32),
            vmem((n_sec, 1, 128), f32),
            pltpu.SemaphoreType.DMA((10,)),
            pltpu.SemaphoreType.DMA((2, PSTEPS, side - 1, K)),
            pltpu.SemaphoreType.DMA((2, PSTEPS, K)),
            pltpu.SemaphoreType.DMA((2, PSTEPS, K)),
            pltpu.SemaphoreType.DMA((2, PSTEPS, side - 1, K)),
            pltpu.SemaphoreType.DMA((2, 2 * PSTEPS, 2, 2)),
            pltpu.SemaphoreType.DMA((2,)),
            pltpu.SemaphoreType.REGULAR((5,)),
        ],
        compiler_params=pltpu.CompilerParams(
            collective_id=0, has_side_effects=True, vmem_limit_bytes=60 * 1024 * 1024
        ),
        name="adjoint",
    )(
        a.reshape(field), g.reshape(field), *[x.reshape(flat) for x in (d, p, js, jn, jc)],
        colour.reshape(8, 128), wall, owner,
    )
    adj, sens = pl.pallas_call(
        finish,
        out_shape=(jax.ShapeDtypeStruct(field, f32), jax.ShapeDtypeStruct((members, SEC_DEV), f32)),
        in_specs=[pl.BlockSpec(memory_space=pltpu.VMEM)] * 2,
        out_specs=(hbm_spec, hbm_spec),
        scratch_shapes=[pltpu.SemaphoreType.DMA((2,))],
        compiler_params=pltpu.CompilerParams(vmem_limit_bytes=1024 * 1024),
        name="finish",
    )(adj, sens)
    return adj.reshape(a.shape), sens


def solution(mesh):
    n_inst, n_space = mesh.shape["inst"], mesh.shape["space"]
    sizes = (32 // n_inst, n_inst, n_space, 4)
    return jax.shard_map(
        functools.partial(on_device, sizes),
        mesh=mesh,
        in_specs=(
            P("inst", None, "space", None, None),
            P("inst", None, "space", None, None),
            P("inst", None, None, "space", None, None),
            P("inst", None, None, "space", None, None),
            P("inst", None, None, "space", None, None),
            P("inst", None, None, "space", None, None),
            P("inst", None, None, "space", None, None),
            P("space", None, None),
            P("inst", None, "space", None),
            P("space", None),
        ),
        out_specs=(P("inst", None, "space", None, None), P("inst", "space")),
        check_vma=False,
    )
```
